1024 devices in a mesh: tower: 2 (over x_lo), blk: 64 (over z, x_hi), mp: 8 (over y, core).
Axes of the slice: x: 4 (x_hi: 2, x_lo: 2; x = x_hi * 2 + x_lo), y: 4, z: 32, core: 2. Of those that a mesh axis runs over, the one named last changes fastest.
Arguments:
- features: bfloat16 [2, 16384, 1152], P('tower', 'blk'), may hold values from -6 to 6
- head: bfloat16 [2, 1152, 1152], P('tower', None, 'mp'), may hold values from -0.1875 to 0.1875
- caption_ids: int32 [16384], replicated, may hold values from 0 to 8191
Outputs:
- head_grad: float32 [2, 1152, 1152], P('tower', 'blk', 'mp')
The draws below stay inside these ranges and needn't reach their ends.
Inputs may be any that keep to these rules, and one draw needn't show every extreme that they name: `caption_ids`: an image and a text with equal caption ids form a positive pair; ids repeat across pairs.
All inputs are finite; a program needn't handle non-finite values.
Results may differ from the reference program's by a relative error of at most 0.003.
Values may be sent and summed in bfloat16 or wider, within the bound.
A program may use at most 32 MiB of HBM per device.

```python
import jax
import jax.numpy as jnp
from jax import lax

D = 1152
E = 1152
ROWS = 256
PAIRS = 16384


def place_ends(entries, key, smallest, top_value):
    longest = entries.shape.index(max(entries.shape))
    spots = []
    for shift in (0, 1):
        where = [jax.random.randint(jax.random.fold_in(key, axis), (), 0, length) for axis, length in enumerate(entries.shape)]
        where[longest] = (where[longest] + shift) % entries.shape[longest]
        spots.append(tuple(where))
    return entries.at[spots[0]].set(smallest).at[spots[1]].set(top_value)


def block_levels(rng, dims, cuts, low, largest):
    def one(dim, shards_of):
        heights = jax.random.uniform(jax.random.fold_in(jax.random.fold_in(rng, 6), dim), (shards_of,), jnp.float32, low / len(cuts), largest / len(cuts))
        return jnp.repeat(jnp.exp(heights), dims[dim] // shards_of).reshape((-1,) + (1,) * (len(dims) - dim - 1))

    loudness = one(*cuts[0])
    for cut in cuts[1:]:
        loudness = loudness * one(*cut)
    return loudness


def scatter_about(own_key, extent, width, most, cuts=(), dtype=jnp.bfloat16):
    factor_of = block_levels(own_key, extent, cuts, -0.22, 0.18) if cuts else 1.0
    entries = jax.random.normal(own_key, extent, jnp.float32) * width * factor_of
    return jnp.minimum(jnp.maximum(entries, -most), most).astype(dtype)


def setup_inputs(seed: int = 0) -> dict:
    keys = jax.random.split(jax.random.key(seed), 4)
    return {
        "features": scatter_about(keys[0], (2, PAIRS, D), 1.0, 6.0, ((0, 2), (1, 64))),
        "head": scatter_about(keys[1], (2, D, E), D ** -0.5, 0.1875, ((0, 2), (2, 8))),
        "caption_ids": place_ends(jax.random.randint(keys[2], (PAIRS,), 0, PAIRS // 2), jax.random.fold_in(keys[2], 1), 0, (PAIRS // 2) - 1).astype(jnp.int32),
    }


LOGIT_SCALE = 10.0
LOGIT_BIAS = -5.0

def pair_gradient(self_tower_rows, opposite_tower, own_ids, partner_ids):
    similarity_logits = LOGIT_SCALE * lax.dot_general(self_tower_rows, opposite_tower, (((1,), (1,)), ((), ())), preferred_element_type=jnp.float32) + LOGIT_BIAS
    label_signs = jnp.where(own_ids[:, None] == partner_ids[None, :], 1.0, -1.0).astype(jnp.float32)
    matching_weights = (-label_signs * jax.nn.sigmoid(-label_signs * similarity_logits)).astype(jnp.bfloat16)
    return LOGIT_SCALE * jnp.dot(matching_weights, opposite_tower, preferred_element_type=jnp.float32)

def embedding_grads(own, opposite_tower, caption_ids):
    blocks = own.shape[0] // ROWS
    own_blocks = own.reshape(blocks, ROWS, own.shape[1])
    id_blocks = caption_ids.reshape(blocks, ROWS)

    def one_block(pieces):
        return pair_gradient(pieces[0], opposite_tower, pieces[1], caption_ids)
    return lax.map(one_block, (own_blocks, id_blocks)).reshape(own.shape[0], own.shape[1])

def reference(features, head, caption_ids):
    output_width = head.shape[2]
    projected = []
    norm_factors = []
    embedded = []
    for tower_number in range(2):
        rounded = lax.optimization_barrier(jnp.dot(features[tower_number], head[tower_number], preferred_element_type=jnp.float32).astype(jnp.bfloat16))
        values = rounded.astype(jnp.float32)
        norm_factor = lax.rsqrt(lax.optimization_barrier(jnp.mean(values * values, axis=1, keepdims=True)) + 1e-06)
        projected.append(values)
        norm_factors.append(norm_factor)
        embedded.append((values * norm_factor * output_width ** (-0.5)).astype(jnp.bfloat16))
    gradients = [embedding_grads(embedded[0], embedded[1], caption_ids), embedding_grads(embedded[1], embedded[0], caption_ids)]
    results = []
    for tower_number in range(2):
        values = projected[tower_number]
        norm_factor = norm_factors[tower_number]
        gradient = gradients[tower_number]
        inner_sum = lax.optimization_barrier(jnp.sum(values * gradient, axis=1, keepdims=True))
        back_rows = (norm_factor * output_width ** (-0.5) * gradient - norm_factor ** 3 * inner_sum * output_width ** (-1.5) * values).astype(jnp.bfloat16)
        results.append(lax.dot_general(features[tower_number], back_rows, (((0,), (0,)), ((), ())), preferred_element_type=jnp.float32))
    return jnp.stack(results)
```

```python
import jax
import jax.numpy as jnp
from jax import lax
from jax.experimental import pallas as pl
from jax.experimental.pallas import tpu as pltpu
from jax.sharding import PartitionSpec as P

MESH = pl.DeviceIdType.MESH
DMA = pltpu.SemaphoreType.DMA
F32, BF16 = jnp.float32, jnp.bfloat16

LOGIT_SCALE = 10.0
LOGIT_BIAS = -5.0
D = E = 1152
ROWS = 256
NZ, NY, NM = 32, 4, 8
SL = ROWS // NM
CH = 2 * SL
COLS = E // NM
STRIP = D // (2 * NZ)
PAD = 24
SUB = 4
SR = CH // SUB
HOPS = NZ // 2
INV = E ** -0.5


def copy_to(src, dst, send, recv, target):
    return pltpu.make_async_remote_copy(
        src_ref=src, dst_ref=dst, send_sem=send, recv_sem=recv, device_id=target, device_id_type=MESH
    )


def kernel(f_ref, h_ref, ids_ref, out_ref,
           wide, pieces, opp_in, own_in, ring, own_rows, own_emb, own_proj, opp_ids, own_ids,
           grad, grad_out, grad_in, strips, strips_out, back_out, back_in, part_out, part_in,
           proj_s, proj_r, emb_s, emb_r, ring_s, ring_r, sib_s, sib_r, strip_s, strip_r,
           grad_s, grad_r, back_s, back_r, part_s, part_r):
    k = lax.axis_index("tower")
    b = lax.axis_index("blk")
    m = lax.axis_index("mp")
    z, xh = b // 2, lax.rem(b, 2)
    y, c = m // 2, lax.rem(m, 2)
    q = xh * NM + m

    def at(tower, plane, half, unit):
        return (tower, plane * 2 + half, unit)

    def in_plane(d):
        other = lax.rem(q + d, 2 * NM)
        return other // NM, lax.rem(other, NM)

    sibling = at(k, z, xh, m + 1 - 2 * c)
    after = at(k, lax.rem(z + 1 + (NZ - 2) * c, NZ), xh, m)
    before = at(k, lax.rem(z + NZ - 1 - (NZ - 2) * c, NZ), xh, m)

    barrier = pltpu.get_barrier_semaphore()

    def greet(target):
        pl.semaphore_signal(barrier, inc=1, device_id=target, device_id_type=MESH)

    def greet_plane(d, carry):
        half, unit = in_plane(d)
        greet(at(k, z, half, unit))
        return carry

    def greet_tower(j, carry):
        greet(at(1 - k, z, xh, j))
        return carry

    def greet_far(d, carry):
        greet(at(k, lax.rem(z + d, NZ), xh, m))
        return carry

    greet(after)
    greet(before)
    lax.fori_loop(1, 2 * NM, greet_plane, 0)
    lax.fori_loop(0, NM, greet_tower, 0)

    wide[...] = jnp.zeros_like(wide)
    wide[:, 0:COLS] = jnp.dot(f_ref[...], h_ref[...], preferred_element_type=F32)
    shifted = pltpu.roll(wide[...], (COLS - 128) * m, 1)
    pieces[...] = shifted.astype(BF16).reshape(NM, SL, 256)
    pl.semaphore_wait(barrier, 2 * NM - 1 + NM + 2)

    def opp_copy(d):
        j = lax.rem(m + d, NM)
        return copy_to(pieces.at[j], opp_in.at[m], proj_s.at[0, d], proj_r.at[0, d], at(1 - k, z, xh, j))

    def own_copy(d):
        j = lax.rem(m + d, NM)
        return copy_to(pieces.at[j], own_in.at[m], proj_s.at[1, d], proj_r.at[1, d], at(k, z, xh, j))

    def send_opp(d, carry):
        opp_copy(d).start()
        return carry

    def send_own(d, carry):
        own_copy(d).start()
        return carry

    lax.fori_loop(0, NM, send_opp, 0)
    lax.fori_loop(1, NM, send_own, 0)
    own_in[m] = pieces[m]

    lane = lax.broadcasted_iota(jnp.int32, (1, 128), 1)
    odd = lax.rem(y, 2) == 1

    def id_row(plane):
        return ids_ref[pl.ds(plane * 4 + xh * 2 + y // 2, 1), :]

    def fill_ids(p, carry):
        left = id_row(lax.rem(z + p, NZ))
        right = id_row(lax.rem(z + NZ - 1 - p, NZ))
        low = jnp.where(odd, pltpu.roll(left, 64, 1), left)
        high = jnp.where(odd, right, pltpu.roll(right, 64, 1))
        opp_ids[pl.ds(p, 1), :] = jnp.where(lane < 64, low, high)
        return carry

    lax.fori_loop(0, HOPS, fill_ids, 0)
    for half in range(2):
        row = ids_ref[pl.ds(z * 4 + 2 * c + half, 1), :]
        own_ids[half * 128:(half + 1) * 128, :] = jnp.broadcast_to(row, (128, 128)).T

    def assemble(slots):
        tiles = [slots[0, :, 0:128]]
        for t in range(1, NM):
            tiles.append(slots[t, :, 0:128] + slots[t - 1, :, 128:256])
        tiles.append(slots[NM - 1, :, 128:256])
        return jnp.concatenate(tiles, axis=1)

    def norm_of(values):
        return lax.rsqrt(jnp.mean(values * values, axis=1, keepdims=True) + 1e-06)

    def embed(projected):
        values = projected.astype(F32)
        return (values * norm_of(values) * INV).astype(BF16)

    def recv_opp(d, carry):
        opp_copy(d).wait_recv()
        return carry

    def recv_own(d, carry):
        own_copy(d).wait_recv()
        return carry

    def slot(s):
        return jnp.maximum(2 * s - 1 + c, 0)

    def hop(s, i):
        rows = pl.ds(pl.multiple_of(i * SR, SR), SR)
        return copy_to(ring.at[slot(s), rows], ring.at[slot(s + 1), rows], ring_s.at[s, i], ring_r.at[s, i], after)

    def share(s):
        return copy_to(ring.at[slot(s)], ring.at[slot(s)], sib_s.at[s], sib_r.at[s], sibling)

    def share_half(s, index):
        rows = pl.ds(pl.multiple_of(c * SL, SL), SL)
        return copy_to(ring.at[index, rows], ring.at[index, rows], sib_s.at[s], sib_r.at[s], sibling)

    def order(i):
        return lax.rem(2 * c + i, SUB)

    lax.fori_loop(0, NM, recv_opp, 0)
    ring[0, pl.ds(pl.multiple_of(c * SL, SL), SL), :] = embed(assemble(opp_in))
    share_half(0, 0).start()
    hop(0, order(0)).start()
    hop(0, order(1)).start()

    lax.fori_loop(1, NM, recv_own, 0)
    own_proj[...] = assemble(own_in)
    own_rows[...] = embed(own_proj[...])

    share_half(0, 0).wait_recv()
    hop(0, order(2)).start()
    hop(0, order(3)).start()

    def emb_copy(dx, dy):
        target = at(k, z, lax.rem(xh + dx, 2), lax.rem(y + dy, NY) * 2 + xh)
        return copy_to(own_rows, own_emb.at[m], emb_s.at[dx, dy], emb_r.at[c, dy], target)

    def emb_wait(core, dy):
        copy_to(own_rows, own_emb.at[0], emb_s.at[0, 0], emb_r.at[core, dy], sibling).wait_recv()

    mine = c == xh

    @pl.when(mine)
    def _():
        own_emb[m] = own_rows[...]

    @pl.when(jnp.logical_not(mine))
    def _():
        emb_copy(0, 0).start()

    for dy in range(1, NY):
        emb_copy(0, dy).start()
    for dy in range(NY):
        emb_copy(1, dy).start()

    def strip_columns(half):
        for part in range(3):
            n = lax.broadcasted_iota(jnp.int32, (256, 1), 0) + part * 256
            plane = (n * 2731) >> 16
            r = n - plane * PAD
            wanted = jnp.where(r < STRIP, plane * (2 * STRIP) + half * STRIP + r, -1)
            pick = (lax.broadcasted_iota(jnp.int32, (256, D), 1) == wanted).astype(BF16)
            yield part, lax.dot_general(
                pick, f_ref[...], (((1,), (1,)), ((), ())), preferred_element_type=F32
            ).astype(BF16)

    for part, value in strip_columns(1 - xh):
        strips_out[part * 256:(part + 1) * 256, :] = value
    strip_copy = copy_to(strips_out, strips.at[1], strip_s, strip_r, at(k, z, 1 - xh, m))
    strip_copy.start()
    for part, value in strip_columns(xh):
        strips[0, part * 256:(part + 1) * 256, :] = value
    grad[...] = jnp.zeros_like(grad)

    def emb_ready():
        for core in range(2):
            for dy in range(NY):
                if dy == 0:
                    @pl.when(jnp.logical_not(jnp.logical_and(mine, core == c)))
                    def _(core=core):
                        emb_wait(core, 0)
                else:
                    emb_wait(core, dy)

    def forward(s):
        for i in range(SUB):
            hop(s - 1, order(i)).wait_recv()
            hop(s, order(i)).start()
        share(s).start()

    def batch(j):
        opposite = ring[pl.ds(4 * j, 4)].reshape(4 * CH, E)
        own = own_emb[...].reshape(ROWS, E)
        logits = LOGIT_SCALE * lax.dot_general(
            own, opposite, (((1,), (1,)), ((), ())), preferred_element_type=F32
        ) + LOGIT_BIAS
        partner = opp_ids[pl.ds(2 * j, 2), :]
        same = jnp.concatenate([own_ids[...] == partner[0:1], own_ids[...] == partner[1:2]], axis=1)
        sign = jnp.where(same, 1.0, -1.0)
        weights = (-sign / (1.0 + jnp.exp(sign * logits))).astype(BF16)
        grad[...] += jnp.dot(weights, opposite, preferred_element_type=F32)

    forward(1)
    forward(2)
    emb_ready()

    def two_hops(t, carry):
        forward(2 * t + 1)
        share(2 * t - 1).wait_recv()
        share(2 * t).wait_recv()
        batch(t - 1)
        forward(2 * t + 2)
        return carry

    lax.fori_loop(1, HOPS // 2 - 1, two_hops, 0)

    last = HOPS - 1

    def last_hop(i):
        rows = pl.ds(pl.multiple_of(i * SR, SR), SR)
        return copy_to(ring.at[slot(last), rows], ring.at[2 * HOPS - 1, rows],
                       ring_s.at[last, i], ring_r.at[last, i], after)

    for i in range(SUB):
        hop(last - 1, order(i)).wait_recv()
        if i < SUB // 2:
            last_hop(order(i)).start()
    share(last).start()
    share(last - 2).wait_recv()
    share(last - 1).wait_recv()
    batch(HOPS // 2 - 2)
    for i in range(SUB // 2):
        last_hop(order(i)).wait_recv()
    share_half(HOPS, 2 * HOPS - 1).start()
    share(last).wait_recv()
    share_half(HOPS, 2 * HOPS - 1).wait_recv()
    batch(HOPS // 2 - 1)

    grad_out[...] = (LOGIT_SCALE * grad[...]).astype(BF16).reshape(NM, SL, E)

    def grad_copy(core, dy):
        unit = lax.rem(y + dy, NY) * 2 + core
        return copy_to(grad_out.at[unit], grad_in.at[xh * NY + dy], grad_s.at[core, dy],
                       grad_r.at[xh, dy], at(k, z, c, unit))

    def grad_wait(half, dy):
        copy_to(grad_out.at[0], grad_in.at[0], grad_s.at[0, 0], grad_r.at[half, dy], sibling).wait_recv()

    def grad_all(act):
        for dy in (2, 1, 3, 0):
            for core in range(2):
                if dy == 0:
                    @pl.when(jnp.logical_not(jnp.logical_and(mine, core == c)))
                    def _(core=core):
                        act(grad_copy(core, 0))
                else:
                    act(grad_copy(core, dy))

    grad_all(lambda copy: copy.start())

    @pl.when(mine)
    def _():
        grad_in[xh * NY] = grad_out[m]

    values = own_proj[...].astype(F32)
    norm = norm_of(values)
    for half in range(2):
        for dy in range(NY):
            if dy == 0:
                @pl.when(jnp.logical_not(jnp.logical_and(mine, xh == half)))
                def _(half=half):
                    grad_wait(half, 0)
            else:
                grad_wait(half, dy)
    gradient = grad_in[0].astype(F32)
    for i in range(1, 2 * NY):
        gradient = gradient + grad_in[i].astype(F32)

    inner = jnp.sum(values * gradient, axis=1, keepdims=True)
    back = (norm * INV * gradient - norm ** 3 * inner * E ** -1.5 * values).astype(BF16)
    for t in range(NM):
        back_out[t] = back[:, t * 128:t * 128 + 256]

    def back_copy(d):
        half, unit = in_plane(d)
        return copy_to(back_out.at[unit], back_in.at[q], back_s.at[d], back_r.at[d], at(k, z, half, unit))

    def send_back(d, carry):
        back_copy(d).start()
        return carry

    def recv_back(d, carry):
        back_copy(d).wait_recv()
        return carry

    lax.fori_loop(1, 2 * NM, send_back, 0)
    back_in[q] = back_out[m]
    strip_copy.wait_recv()
    lax.fori_loop(1, 2 * NM, recv_back, 0)

    own_back = back_in[pl.ds(xh * NM, NM)].reshape(ROWS, 256)
    other_back = back_in[pl.ds((1 - xh) * NM, NM)].reshape(ROWS, 256)
    head_part = jnp.dot(strips[0], own_back, preferred_element_type=F32)
    head_part += jnp.dot(strips[1], other_back, preferred_element_type=F32)
    head_part = pltpu.roll(head_part, lax.rem(256 - (COLS - 128) * m, 256), 1)
    extra = jnp.where(lane < COLS - 128, head_part[:, 128:256], 0.0)
    extra = pltpu.roll(extra, 0, 1, stride=COLS - 128, stride_axis=0)
    extra = jnp.sum(extra.reshape(NZ, PAD // 8, 8, 128), axis=2)
    packed = head_part[:, 0:128].reshape(NZ, PAD, 128)
    r = lax.broadcasted_iota(jnp.int32, (NZ, PAD, 128), 1)
    for g in range(PAD // 8):
        packed = jnp.where(r == STRIP + g, extra[:, g:g + 1, :], packed)
    part_out[:, 0:PAD, :] = packed.astype(BF16)
    part_out[:, PAD:32, :] = jnp.zeros((NZ, 32 - PAD, 128), BF16)

    def part_copy(d):
        plane = lax.rem(z + d, NZ)
        return copy_to(part_out.at[plane], part_in.at[d], part_s.at[d], part_r.at[d], at(k, plane, xh, m))

    def send_part(i, carry):
        part_copy(HOPS - i).start()

        @pl.when(i > 0)
        def _():
            part_copy(HOPS + i).start()
        return carry

    def recv_part(d, carry):
        part_copy(d).wait_recv()
        return carry

    lax.fori_loop(0, HOPS, send_part, 0)
    part_in[0] = part_out[z]
    lax.fori_loop(1, NZ, recv_part, 0)
    total = part_in[0].astype(F32)
    for d in range(1, NZ):
        total = total + part_in[d].astype(F32)
    out_ref[:, 0:128] = total[0:STRIP, :]
    spread = jnp.concatenate(
        [jnp.broadcast_to(total[STRIP + g:STRIP + g + 1, :], (8, 128)) for g in range(PAD // 8)], axis=0
    )
    row = lax.rem(lax.broadcasted_iota(jnp.int32, (PAD, 128), 0), 8)
    tail = spread
    for j in range(1, 8):
        tail = jnp.where(row == j, pltpu.roll(spread, 128 - (COLS - 128) * j, 1), tail)
    out_ref[:, 128:COLS] = tail[0:STRIP, 0:COLS - 128]

    def sent_proj(d, carry):
        opp_copy(d).wait_send()

        @pl.when(d > 0)
        def _():
            own_copy(d).wait_send()
        return carry

    def sent_hops(s, carry):
        for i in range(SUB):
            hop(s, i).wait_send()
        share(s + 1).wait_send()
        return carry

    def sent_back(d, carry):
        back_copy(d).wait_send()
        return carry

    def sent_part(d, carry):
        part_copy(d).wait_send()
        return carry

    lax.fori_loop(0, NM, sent_proj, 0)
    share_half(0, 0).wait_send()
    lax.fori_loop(0, last, sent_hops, 0)
    for i in range(SUB // 2):
        last_hop(order(i)).wait_send()
    share_half(HOPS, 2 * HOPS - 1).wait_send()

    @pl.when(jnp.logical_not(mine))
    def _():
        emb_copy(0, 0).wait_send()

    for dy in range(1, NY):
        emb_copy(0, dy).wait_send()
    for dy in range(NY):
        emb_copy(1, dy).wait_send()
    strip_copy.wait_send()
    grad_all(lambda copy: copy.wait_send())
    lax.fori_loop(1, 2 * NM, sent_back, 0)
    lax.fori_loop(1, NZ, sent_part, 0)


def per_device(features, head, caption_ids):
    vmem = pl.BlockSpec(memory_space=pltpu.VMEM)
    flops = 2 * ROWS * D * COLS + 4 * ROWS * NZ * CH * E + 4 * NZ * PAD * ROWS * 256
    out = pl.pallas_call(
        kernel,
        out_shape=jax.ShapeDtypeStruct((STRIP, COLS), F32),
        in_specs=[vmem] * 3,
        out_specs=vmem,
        scratch_shapes=[
            pltpu.VMEM((ROWS, 256), F32),
            pltpu.VMEM((NM, SL, 256), BF16),
            pltpu.VMEM((NM, SL, 256), BF16),
            pltpu.VMEM((NM, SL, 256), BF16),
            pltpu.VMEM((NZ, CH, E), BF16),
            pltpu.VMEM((SL, E), BF16),
            pltpu.VMEM((NM, SL, E), BF16),
            pltpu.VMEM((SL, E), BF16),
            pltpu.VMEM((HOPS, 128), jnp.int32),
            pltpu.VMEM((ROWS, 128), jnp.int32),
            pltpu.VMEM((ROWS, E), F32),
            pltpu.VMEM((NM, SL, E), BF16),
            pltpu.VMEM((2 * NY, SL, E), BF16),
            pltpu.VMEM((2, NZ * PAD, ROWS), BF16),
            pltpu.VMEM((NZ * PAD, ROWS), BF16),
            pltpu.VMEM((NM, SL, 256), BF16),
            pltpu.VMEM((2 * NM, SL, 256), BF16),
            pltpu.VMEM((NZ, 32, 128), BF16),
            pltpu.VMEM((NZ, 32, 128), BF16),
            DMA((2, NM)), DMA((2, NM)),
            DMA((2, NY)), DMA((2, NY)),
            DMA((HOPS, SUB)), DMA((HOPS, SUB)),
            DMA((HOPS + 1,)), DMA((HOPS + 1,)),
            DMA, DMA,
            DMA((2, NY)), DMA((2, NY)),
            DMA((2 * NM,)), DMA((2 * NM,)),
            DMA((NZ,)), DMA((NZ,)),
        ],
        compiler_params=pltpu.CompilerParams(
            collective_id=0, has_side_effects=True, vmem_limit_bytes=40 << 20
        ),
        cost_estimate=pl.CostEstimate(flops=flops, bytes_accessed=2 << 20, transcendentals=ROWS * NZ * CH),
    )(features[0], head[0], caption_ids.reshape(128, 128))
    return out[None]


def solution(mesh):
    in_specs = (P("tower", "blk", None), P("tower", None, "mp"), P())
    out_specs = P("tower", "blk", "mp")
    return jax.shard_map(
        per_device, mesh=mesh, in_specs=in_specs, out_specs=out_specs, check_vma=False
    )
```

```python
import jax
import jax.numpy as jnp
from jax import lax
from jax.experimental import pallas as pl
from jax.experimental.pallas import tpu as pltpu
from jax.sharding import PartitionSpec as P

MESH = pl.DeviceIdType.MESH
DMA = pltpu.SemaphoreType.DMA
F32, BF16 = jnp.float32, jnp.bfloat16

LOGIT_SCALE = 10.0
LOGIT_BIAS = -5.0
D = E = 1152
ROWS = 256
NZ, NY, NM = 32, 4, 8
SL = ROWS // NM
CH = 2 * SL
COLS = E // NM
STRIP = D // (2 * NZ)
PAD = 24
SUB = 4
SR = CH // SUB
HOPS = NZ // 2
JUMP = 4
GROUP = 4
GROUPS = NZ // GROUP
INV = E ** -0.5


def copy_to(src, dst, send, recv, target):
    return pltpu.make_async_remote_copy(
        src_ref=src, dst_ref=dst, send_sem=send, recv_sem=recv, device_id=target, device_id_type=MESH
    )


def kernel(f_ref, h_ref, ids_ref, out_ref,
           rows_in, head_in, ids_in, pieces, opp_in, own_in, ring, own_rows, own_emb, own_proj, opp_ids, own_ids,
           grad, grad_out, grad_in, strips, strips_out, back_out, back_in, part_out, part_in,
           sum_out, sum_in,
           in_s, proj_s, proj_r, emb_s, emb_r, ring_s, ring_r, sib_s, sib_r, strip_s, strip_r,
           grad_s, grad_r, back_s, back_r, part_s, part_r, sum_s, sum_r):
    k = lax.axis_index("tower")
    b = lax.axis_index("blk")
    m = lax.axis_index("mp")
    z, xh = b // 2, lax.rem(b, 2)
    y, c = m // 2, lax.rem(m, 2)
    q = xh * NM + m

    def at(tower, plane, half, unit):
        return (tower, plane * 2 + half, unit)

    def in_plane(d):
        other = lax.rem(q + d, 2 * NM)
        return other // NM, lax.rem(other, NM)

    sibling = at(k, z, xh, m + 1 - 2 * c)
    after = at(k, lax.rem(z + 1 + (NZ - 2) * c, NZ), xh, m)
    before = at(k, lax.rem(z + NZ - 1 - (NZ - 2) * c, NZ), xh, m)
    ahead = at(k, lax.rem(z + JUMP + (NZ - 2 * JUMP) * c, NZ), xh, m)
    behind = at(k, lax.rem(z + NZ - JUMP - (NZ - 2 * JUMP) * c, NZ), xh, m)

    barrier = pltpu.get_barrier_semaphore()

    def greet(target):
        pl.semaphore_signal(barrier, inc=1, device_id=target, device_id_type=MESH)

    def greet_plane(d, carry):
        half, unit = in_plane(d)
        greet(at(k, z, half, unit))
        return carry

    def greet_tower(j, carry):
        greet(at(1 - k, z, xh, j))
        return carry

    greet(after)
    greet(before)
    greet(ahead)
    greet(behind)
    lax.fori_loop(1, 2 * NM, greet_plane, 0)
    lax.fori_loop(0, NM, greet_tower, 0)

    shift = (COLS - 128) * m
    rows_copy = pltpu.make_async_copy(f_ref, rows_in, in_s.at[0])
    rows_copy.start()
    ids_copy = pltpu.make_async_copy(ids_ref, ids_in, in_s.at[1])
    ids_copy.start()
    head_in[...] = jnp.zeros_like(head_in)
    head_copy = pltpu.make_async_copy(h_ref, head_in.at[pl.ds(pl.multiple_of(shift, 16), COLS)], in_s.at[2])
    head_copy.start()
    rows_copy.wait()
    head_copy.wait()
    pieces[...] = lax.dot_general(
        rows_in[...], head_in[...], (((1,), (1,)), ((), ())), preferred_element_type=F32
    ).astype(BF16).reshape(NM, SL, 256)
    pl.semaphore_wait(barrier, 2 * NM - 1 + NM + 4)

    def opp_copy(d):
        j = lax.rem(m + d, NM)
        return copy_to(pieces.at[j], opp_in.at[m], proj_s.at[0, d], proj_r.at[0, d], at(1 - k, z, xh, j))

    def own_copy(d):
        j = lax.rem(m + d, NM)
        return copy_to(pieces.at[j], own_in.at[m], proj_s.at[1, d], proj_r.at[1, d], at(k, z, xh, j))

    def send_opp(d, carry):
        opp_copy(d).start()
        return carry

    def send_own(d, carry):
        own_copy(d).start()
        return carry

    lax.fori_loop(0, NM, send_opp, 0)
    lax.fori_loop(1, NM, send_own, 0)
    own_in[m] = pieces[m]

    lane = lax.broadcasted_iota(jnp.int32, (1, 128), 1)
    odd = lax.rem(y, 2) == 1

    def id_row(plane):
        return ids_in[pl.ds(plane * 4 + xh * 2 + y // 2, 1), :]

    def fill_ids(p, carry):
        left = id_row(lax.rem(z + p, NZ))
        right = id_row(lax.rem(z + NZ - 1 - p, NZ))
        low = jnp.where(odd, pltpu.roll(left, 64, 1), left)
        high = jnp.where(odd, right, pltpu.roll(right, 64, 1))
        opp_ids[pl.ds(p, 1), :] = jnp.where(lane < 64, low, high)
        return carry

    ids_copy.wait()
    lax.fori_loop(0, HOPS, fill_ids, 0)
    for half in range(2):
        row = ids_in[pl.ds(z * 4 + 2 * c + half, 1), :]
        own_ids[half * 128:(half + 1) * 128, :] = jnp.broadcast_to(row, (128, 128)).T

    def assemble(slots):
        tiles = [slots[0, :, 0:128]]
        for t in range(1, NM):
            tiles.append(slots[t, :, 0:128] + slots[t - 1, :, 128:256])
        tiles.append(slots[NM - 1, :, 128:256])
        return jnp.concatenate(tiles, axis=1)

    def norm_of(values):
        return lax.rsqrt(jnp.mean(values * values, axis=1, keepdims=True) + 1e-06)

    def embed(projected):
        values = projected.astype(F32)
        return (values * norm_of(values) * INV).astype(BF16)

    def recv_opp(d, carry):
        opp_copy(d).wait_recv()
        return carry

    def recv_own(d, carry):
        own_copy(d).wait_recv()
        return carry

    def slot(s):
        return jnp.maximum(2 * s - 1 + c, 0)

    def hop(s, i):
        rows = pl.ds(pl.multiple_of(i * SR, SR), SR)
        return copy_to(ring.at[slot(s), rows], ring.at[slot(s + 1), rows], ring_s.at[s, i], ring_r.at[s, i], after)

    def jump(i):
        rows = pl.ds(pl.multiple_of(i * SR, SR), SR)
        return copy_to(ring.at[0, rows], ring.at[slot(JUMP), rows], ring_s.at[JUMP - 1, i], ring_r.at[JUMP - 1, i], ahead)

    def share(s):
        return copy_to(ring.at[slot(s)], ring.at[slot(s)], sib_s.at[s], sib_r.at[s], sibling)

    def share_half(s, index):
        rows = pl.ds(pl.multiple_of(c * SL, SL), SL)
        return copy_to(ring.at[index, rows], ring.at[index, rows], sib_s.at[s], sib_r.at[s], sibling)

    def order(i):
        return lax.rem(2 * c + i, SUB)

    lax.fori_loop(0, NM, recv_opp, 0)
    ring[0, pl.ds(pl.multiple_of(c * SL, SL), SL), :] = embed(assemble(opp_in))
    share_half(0, 0).start()
    jump(order(0)).start()
    jump(order(1)).start()
    hop(0, order(0)).start()
    hop(0, order(1)).start()

    lax.fori_loop(1, NM, recv_own, 0)
    own_proj[...] = assemble(own_in)
    own_rows[...] = embed(own_proj[...])

    share_half(0, 0).wait_recv()
    jump(order(2)).start()
    jump(order(3)).start()
    hop(0, order(2)).start()
    hop(0, order(3)).start()

    def emb_copy(dx, dy):
        target = at(k, z, lax.rem(xh + dx, 2), lax.rem(y + dy, NY) * 2 + xh)
        return copy_to(own_rows, own_emb.at[m], emb_s.at[dx, dy], emb_r.at[c, dy], target)

    def emb_wait(core, dy):
        copy_to(own_rows, own_emb.at[0], emb_s.at[0, 0], emb_r.at[core, dy], sibling).wait_recv()

    mine = c == xh

    @pl.when(mine)
    def _():
        own_emb[m] = own_rows[...]

    @pl.when(jnp.logical_not(mine))
    def _():
        emb_copy(0, 0).start()

    for dy in range(1, NY):
        emb_copy(0, dy).start()
    for dy in range(NY):
        emb_copy(1, dy).start()

    def strip_columns(half):
        for part in range(3):
            n = lax.broadcasted_iota(jnp.int32, (256, 1), 0) + part * 256
            place = (n * 2731) >> 16
            r = n - place * PAD
            plane = (place & (GROUPS - 1)) * GROUP + (place >> 3)
            wanted = jnp.where(r < STRIP, plane * (2 * STRIP) + half * STRIP + r, -1)
            pick = (lax.broadcasted_iota(jnp.int32, (256, D), 1) == wanted).astype(BF16)
            yield part, lax.dot_general(
                pick, rows_in[...], (((1,), (1,)), ((), ())), preferred_element_type=F32
            ).astype(BF16)

    for part, value in strip_columns(1 - xh):
        strips_out[part * 256:(part + 1) * 256, :] = value
    strip_copy = copy_to(strips_out, strips.at[1], strip_s, strip_r, at(k, z, 1 - xh, m))
    strip_copy.start()
    for part, value in strip_columns(xh):
        strips[0, part * 256:(part + 1) * 256, :] = value
    grad[...] = jnp.zeros_like(grad)

    def emb_ready():
        for core in range(2):
            for dy in range(NY):
                if dy == 0:
                    @pl.when(jnp.logical_not(jnp.logical_and(mine, core == c)))
                    def _(core=core):
                        emb_wait(core, 0)
                else:
                    emb_wait(core, dy)

    def forward(s):
        for i in range(SUB):
            hop(s - 1, order(i)).wait_recv()
            hop(s, order(i)).start()
        share(s).start()

    def end_of_chain(s):
        for i in range(SUB):
            hop(s - 1, order(i)).wait_recv()
        share(s).start()

    def batch(j):
        opposite = ring[pl.ds(4 * j, 4)].reshape(4 * CH, E)
        own = own_emb[...].reshape(ROWS, E)
        logits = LOGIT_SCALE * lax.dot_general(
            own, opposite, (((1,), (1,)), ((), ())), preferred_element_type=F32
        ) + LOGIT_BIAS
        partner = opp_ids[pl.ds(2 * j, 2), :]
        same = jnp.concatenate([own_ids[...] == partner[0:1], own_ids[...] == partner[1:2]], axis=1)
        sign = jnp.where(same, 1.0, -1.0)
        weights = (-sign / (1.0 + jnp.exp(sign * logits))).astype(BF16)
        grad[...] += jnp.dot(weights, opposite, preferred_element_type=F32)

    for t in range(1, JUMP):
        if t < JUMP - 1:
            forward(t)
        else:
            end_of_chain(t)
        forward(JUMP - 1 + t)
    emb_ready()

    def arrived(j):
        share(2 * j + 1).wait_recv()
        share(2 * j + 2).wait_recv()

    def one_hop(t, carry):
        forward(JUMP - 1 + t)
        arrived(t - JUMP)
        batch(t - JUMP)
        return carry

    def two_hops(u, carry):
        forward(2 * u + JUMP - 1)
        arrived(u)
        batch(u)
        forward(2 * u + JUMP)
        return carry

    lax.fori_loop(JUMP, 2 * JUMP, one_hop, 0)
    lax.fori_loop(JUMP, HOPS // 2 - 2, two_hops, 0)

    last = HOPS - 1

    def last_hop(i):
        rows = pl.ds(pl.multiple_of(i * SR, SR), SR)
        return copy_to(ring.at[slot(last), rows], ring.at[2 * HOPS - 1, rows],
                       ring_s.at[last, i], ring_r.at[last, i], after)

    for i in range(SUB):
        hop(last - 1, order(i)).wait_recv()
        if i < SUB // 2:
            last_hop(order(i)).start()
    share(last).start()
    arrived(HOPS // 2 - 2)
    batch(HOPS // 2 - 2)
    for i in range(SUB // 2):
        last_hop(order(i)).wait_recv()
    share_half(HOPS, 2 * HOPS - 1).start()
    share(last).wait_recv()
    share_half(HOPS, 2 * HOPS - 1).wait_recv()
    batch(HOPS // 2 - 1)

    grad_out[...] = (LOGIT_SCALE * grad[...]).astype(BF16).reshape(NM, SL, E)

    def grad_copy(core, dy):
        unit = lax.rem(y + dy, NY) * 2 + core
        return copy_to(grad_out.at[unit], grad_in.at[xh * NY + dy], grad_s.at[core, dy],
                       grad_r.at[xh, dy], at(k, z, c, unit))

    def grad_wait(half, dy):
        copy_to(grad_out.at[0], grad_in.at[0], grad_s.at[0, 0], grad_r.at[half, dy], sibling).wait_recv()

    def grad_all(act):
        for dy in (2, 1, 3, 0):
            for core in range(2):
                if dy == 0:
                    @pl.when(jnp.logical_not(jnp.logical_and(mine, core == c)))
                    def _(core=core):
                        act(grad_copy(core, 0))
                else:
                    act(grad_copy(core, dy))

    grad_all(lambda copy: copy.start())

    @pl.when(mine)
    def _():
        grad_in[xh * NY] = grad_out[m]

    values = own_proj[...].astype(F32)
    norm = norm_of(values)
    for half in range(2):
        for dy in range(NY):
            if dy == 0:
                @pl.when(jnp.logical_not(jnp.logical_and(mine, xh == half)))
                def _(half=half):
                    grad_wait(half, 0)
            else:
                grad_wait(half, dy)
    gradient = grad_in[0].astype(F32)
    for i in range(1, 2 * NY):
        gradient = gradient + grad_in[i].astype(F32)

    inner = jnp.sum(values * gradient, axis=1, keepdims=True)
    back = (norm * INV * gradient - norm ** 3 * inner * E ** -1.5 * values).astype(BF16)
    for t in range(NM):
        back_out[t] = back[:, t * 128:t * 128 + 256]

    def back_copy(d):
        half, unit = in_plane(d)
        return copy_to(back_out.at[unit], back_in.at[q], back_s.at[d], back_r.at[d], at(k, z, half, unit))

    def send_back(d, carry):
        back_copy(d).start()
        return carry

    def recv_back(d, carry):
        back_copy(d).wait_recv()
        return carry

    lax.fori_loop(1, 2 * NM, send_back, 0)
    back_in[q] = back_out[m]
    strip_copy.wait_recv()
    lax.fori_loop(1, 2 * NM, recv_back, 0)

    own_back = back_in[pl.ds(xh * NM, NM)].reshape(ROWS, 256)
    other_back = back_in[pl.ds((1 - xh) * NM, NM)].reshape(ROWS, 256)
    head_part = jnp.dot(strips[0], own_back, preferred_element_type=F32)
    head_part += jnp.dot(strips[1], other_back, preferred_element_type=F32)
    head_part = pltpu.roll(head_part, lax.rem(256 - (COLS - 128) * m, 256), 1)
    extra = jnp.where(lane < COLS - 128, head_part[:, 128:256], 0.0)
    extra = pltpu.roll(extra, 0, 1, stride=COLS - 128, stride_axis=0)
    extra = jnp.sum(extra.reshape(NZ, PAD // 8, 8, 128), axis=2)
    packed = head_part[:, 0:128].reshape(NZ, PAD, 128)
    r = lax.broadcasted_iota(jnp.int32, (NZ, PAD, 128), 1)
    for g in range(PAD // 8):
        packed = jnp.where(r == STRIP + g, extra[:, g:g + 1, :], packed)
    part_out[:, :, 0:PAD, :] = packed.astype(BF16).reshape(GROUP, GROUPS, PAD, 128)
    part_out[:, :, PAD:32, :] = jnp.zeros((GROUP, GROUPS, 32 - PAD, 128), BF16)

    low, high = lax.rem(z, GROUP), z // GROUP

    def part_copy(d):
        place = lax.rem(low + d, GROUP)
        return copy_to(part_out.at[place], part_in.at[d - 1], part_s.at[d], part_r.at[d],
                       at(k, high * GROUP + place, xh, m))

    def sum_copy(d):
        place = lax.rem(high + d, GROUPS)
        return copy_to(sum_out.at[place], sum_in.at[d], sum_s.at[d], sum_r.at[d],
                       at(k, place * GROUP + low, xh, m))

    def sent_proj(d, carry):
        opp_copy(d).wait_send()

        @pl.when(d > 0)
        def _():
            own_copy(d).wait_send()
        return carry

    def sent_hops(s, carry):
        for i in range(SUB):
            hop(s, i).wait_send()
        share(s + 1).wait_send()
        return carry

    def sent_back(d, carry):
        back_copy(d).wait_send()
        return carry

    for d in (2, 1, 3):
        part_copy(d).start()
    lax.fori_loop(0, NM, sent_proj, 0)
    share_half(0, 0).wait_send()
    lax.fori_loop(0, last, sent_hops, 0)
    for i in range(SUB // 2):
        last_hop(order(i)).wait_send()
    share_half(HOPS, 2 * HOPS - 1).wait_send()

    @pl.when(jnp.logical_not(mine))
    def _():
        emb_copy(0, 0).wait_send()

    for dy in range(1, NY):
        emb_copy(0, dy).wait_send()
    for dy in range(NY):
        emb_copy(1, dy).wait_send()
    strip_copy.wait_send()
    grad_all(lambda copy: copy.wait_send())
    lax.fori_loop(1, 2 * NM, sent_back, 0)
    own_part = part_out[low].astype(F32)
    for d in (1, 3, 2):
        part_copy(d).wait_recv()
    summed = own_part
    for d in range(GROUP - 1):
        summed = summed + part_in[d].astype(F32)
    sum_out[...] = summed.astype(BF16)
    for d in (4, 3, 5, 2, 6, 1, 7):
        sum_copy(d).start()
    for d in range(1, GROUP):
        part_copy(d).wait_send()
    for d in range(1, GROUPS):
        sum_copy(d).wait_send()
    total = sum_out[high].astype(F32)
    for d in (1, 7, 2, 6, 3, 5, 4):
        sum_copy(d).wait_recv()
        total = total + sum_in[d].astype(F32)
    out_ref[:, 0:128] = total[0:STRIP, :]
    spread = jnp.concatenate(
        [jnp.broadcast_to(total[STRIP + g:STRIP + g + 1, :], (8, 128)) for g in range(PAD // 8)], axis=0
    )
    row = lax.rem(lax.broadcasted_iota(jnp.int32, (PAD, 128), 0), 8)
    tail = spread
    for j in range(1, 8):
        tail = jnp.where(row == j, pltpu.roll(spread, 128 - (COLS - 128) * j, 1), tail)
    out_ref[:, 128:COLS] = tail[0:STRIP, 0:COLS - 128]


def per_device(features, head, caption_ids):
    vmem = pl.BlockSpec(memory_space=pltpu.VMEM)
    flops = 2 * ROWS * D * COLS + 4 * ROWS * NZ * CH * E + 4 * NZ * PAD * ROWS * 256
    out = pl.pallas_call(
        kernel,
        out_shape=jax.ShapeDtypeStruct((STRIP, COLS), F32),
        in_specs=[pl.BlockSpec(memory_space=pl.ANY)] * 3,
        out_specs=vmem,
        scratch_shapes=[
            pltpu.VMEM((ROWS, D), BF16),
            pltpu.VMEM((256, D), BF16),
            pltpu.VMEM((128, 128), jnp.int32),
            pltpu.VMEM((NM, SL, 256), BF16),
            pltpu.VMEM((NM, SL, 256), BF16),
            pltpu.VMEM((NM, SL, 256), BF16),
            pltpu.VMEM((NZ, CH, E), BF16),
            pltpu.VMEM((SL, E), BF16),
            pltpu.VMEM((NM, SL, E), BF16),
            pltpu.VMEM((SL, E), BF16),
            pltpu.VMEM((HOPS, 128), jnp.int32),
            pltpu.VMEM((ROWS, 128), jnp.int32),
            pltpu.VMEM((ROWS, E), F32),
            pltpu.VMEM((NM, SL, E), BF16),
            pltpu.VMEM((2 * NY, SL, E), BF16),
            pltpu.VMEM((2, NZ * PAD, ROWS), BF16),
            pltpu.VMEM((NZ * PAD, ROWS), BF16),
            pltpu.VMEM((NM, SL, 256), BF16),
            pltpu.VMEM((2 * NM, SL, 256), BF16),
            pltpu.VMEM((GROUP, GROUPS, 32, 128), BF16),
            pltpu.VMEM((GROUP - 1, GROUPS, 32, 128), BF16),
            pltpu.VMEM((GROUPS, 32, 128), BF16),
            pltpu.VMEM((GROUPS, 32, 128), BF16),
            DMA((3,)),
            DMA((2, NM)), DMA((2, NM)),
            DMA((2, NY)), DMA((2, NY)),
            DMA((HOPS, SUB)), DMA((HOPS, SUB)),
            DMA((HOPS + 1,)), DMA((HOPS + 1,)),
            DMA, DMA,
            DMA((2, NY)), DMA((2, NY)),
            DMA((2 * NM,)), DMA((2 * NM,)),
            DMA((GROUP,)), DMA((GROUP,)),
            DMA((GROUPS,)), DMA((GROUPS,)),
        ],
        compiler_params=pltpu.CompilerParams(
            collective_id=0, has_side_effects=True, vmem_limit_bytes=63 << 20
        ),
        cost_estimate=pl.CostEstimate(flops=flops, bytes_accessed=2 << 20, transcendentals=ROWS * NZ * CH),
    )(features[0], head[0].T, caption_ids.reshape(128, 128))
    return out[None]


def solution(mesh):
    in_specs = (P("tower", "blk", None), P("tower", None, "mp"), P())
    out_specs = P("tower", "blk", "mp")
    return jax.shard_map(
        per_device, mesh=mesh, in_specs=in_specs, out_specs=out_specs, check_vma=False
    )
```

```python
import jax
import jax.numpy as jnp
from jax import lax
from jax.experimental import pallas as pl
from jax.experimental.pallas import tpu as pltpu
from jax.sharding import PartitionSpec as P

MESH = pl.DeviceIdType.MESH
DMA = pltpu.SemaphoreType.DMA
F32, BF16 = jnp.float32, jnp.bfloat16

LOGIT_SCALE = 10.0
LOGIT_BIAS = -5.0
D = E = 1152
ROWS = 256
NZ, NY, NM = 32, 4, 8
SL = ROWS // NM
CH = 2 * SL
COLS = E // NM
STRIP = D // (2 * NZ)
PAD = 24
SUB = 4
SR = CH // SUB
HOPS = NZ // 2
JUMP = 8
GROUP = 4
GROUPS = NZ // GROUP
INV = E ** -0.5


def copy_to(src, dst, send, recv, target):
    return pltpu.make_async_remote_copy(
        src_ref=src, dst_ref=dst, send_sem=send, recv_sem=recv, device_id=target, device_id_type=MESH
    )


def kernel(f_ref, h_ref, ids_ref, out_ref,
           rows_in, head_in, ids_in, pieces, opp_in, own_in, ring, own_rows, own_emb, own_proj, opp_ids, own_ids,
           grad, grad_out, grad_in, strips, strips_out, back_out, back_in, part_out, part_in,
           sum_out, sum_in,
           in_s, proj_s, proj_r, emb_s, emb_r, ring_s, ring_r, sib_s, sib_r, strip_s, strip_r,
           grad_s, grad_r, back_s, back_r, part_s, part_r, sum_s, sum_r):
    k = lax.axis_index("tower")
    b = lax.axis_index("blk")
    m = lax.axis_index("mp")
    z, xh = b // 2, lax.rem(b, 2)
    y, c = m // 2, lax.rem(m, 2)
    q = xh * NM + m

    def at(tower, plane, half, unit):
        return (tower, plane * 2 + half, unit)

    def in_plane(d):
        other = lax.rem(q + d, 2 * NM)
        return other // NM, lax.rem(other, NM)

    sibling = at(k, z, xh, m + 1 - 2 * c)
    after = at(k, lax.rem(z + 1 + (NZ - 2) * c, NZ), xh, m)
    before = at(k, lax.rem(z + NZ - 1 - (NZ - 2) * c, NZ), xh, m)
    ahead = at(k, lax.rem(z + JUMP + (NZ - 2 * JUMP) * c, NZ), xh, m)
    behind = at(k, lax.rem(z + NZ - JUMP - (NZ - 2 * JUMP) * c, NZ), xh, m)

    barrier = pltpu.get_barrier_semaphore()

    def greet(target):
        pl.semaphore_signal(barrier, inc=1, device_id=target, device_id_type=MESH)

    def greet_plane(d, carry):
        half, unit = in_plane(d)
        greet(at(k, z, half, unit))
        return carry

    def greet_tower(j, carry):
        greet(at(1 - k, z, c, j))
        return carry

    greet(after)
    greet(before)
    greet(ahead)
    greet(behind)
    lax.fori_loop(1, 2 * NM, greet_plane, 0)
    lax.fori_loop(0, NM, greet_tower, 0)

    shift = (COLS - 128) * m
    rows_copy = pltpu.make_async_copy(f_ref, rows_in, in_s.at[0])
    rows_copy.start()
    ids_copy = pltpu.make_async_copy(ids_ref, ids_in, in_s.at[1])
    ids_copy.start()
    head_in[...] = jnp.zeros_like(head_in)
    head_copy = pltpu.make_async_copy(h_ref, head_in.at[pl.ds(pl.multiple_of(shift, 16), COLS)], in_s.at[2])
    head_copy.start()
    rows_copy.wait()
    head_copy.wait()
    pieces[...] = lax.dot_general(
        rows_in[...], head_in[...], (((1,), (1,)), ((), ())), preferred_element_type=F32
    ).astype(BF16).reshape(NM, SL, 256)
    pl.semaphore_wait(barrier, 2 * NM - 1 + NM + 4)

    def opp_copy(d):
        j = lax.rem(m + d, NM)
        return copy_to(pieces.at[j], opp_in.at[m], proj_s.at[0, d], proj_r.at[0, d],
                       at(1 - k, z, lax.rem(j, 2), (j // 2) * 2 + xh))

    def own_copy(d):
        j = lax.rem(m + d, NM)
        return copy_to(pieces.at[j], own_in.at[m], proj_s.at[1, d], proj_r.at[1, d], at(k, z, xh, j))

    def send_opp(d, carry):
        opp_copy(d).start()
        return carry

    def send_own(d, carry):
        own_copy(d).start()
        return carry

    lax.fori_loop(0, NM, send_opp, 0)
    lax.fori_loop(1, NM, send_own, 0)
    own_in[m] = pieces[m]

    lane = lax.broadcasted_iota(jnp.int32, (1, 128), 1)
    quarter = lax.rem(2 * y + xh, 4) * SL

    def fill_ids(p, carry):
        row = jnp.zeros((1, 128), jnp.int32)
        for place in range(4):
            plane = lax.rem(z + p, NZ) if place < 2 else lax.rem(z + NZ - 1 - p, NZ)
            some = ids_in[pl.ds(plane * 4 + (place % 2) * 2 + y // 2, 1), :]
            some = pltpu.roll(some, lax.rem(128 + place * SL - quarter, 128), 1)
            row = jnp.where(lane // SL == place, some, row)
        opp_ids[pl.ds(p, 1), :] = row
        return carry

    ids_copy.wait()
    lax.fori_loop(0, HOPS, fill_ids, 0)
    for half in range(2):
        row = ids_in[pl.ds(z * 4 + 2 * c + half, 1), :]
        own_ids[half * 128:(half + 1) * 128, :] = jnp.broadcast_to(row, (128, 128)).T

    def strip_columns(half):
        for part in range(3):
            n = lax.broadcasted_iota(jnp.int32, (256, 1), 0) + part * 256
            place = (n * 2731) >> 16
            r = n - place * PAD
            plane = (place & (GROUPS - 1)) * GROUP + (place >> 3)
            wanted = jnp.where(r < STRIP, plane * (2 * STRIP) + half * STRIP + r, -1)
            pick = (lax.broadcasted_iota(jnp.int32, (256, D), 1) == wanted).astype(BF16)
            yield part, lax.dot_general(
                pick, rows_in[...], (((1,), (1,)), ((), ())), preferred_element_type=F32
            ).astype(BF16)

    for part, value in strip_columns(1 - xh):
        strips_out[part * 256:(part + 1) * 256, :] = value
    strip_copy = copy_to(strips_out, strips.at[1], strip_s, strip_r, at(k, z, 1 - xh, m))
    for part, value in strip_columns(xh):
        strips[0, part * 256:(part + 1) * 256, :] = value

    def assemble(slots):
        tiles = [slots[0, :, 0:128]]
        for t in range(1, NM):
            tiles.append(slots[t, :, 0:128] + slots[t - 1, :, 128:256])
        tiles.append(slots[NM - 1, :, 128:256])
        return jnp.concatenate(tiles, axis=1)

    def norm_of(values):
        return lax.rsqrt(jnp.mean(values * values, axis=1, keepdims=True) + 1e-06)

    def embed(projected):
        values = projected.astype(F32)
        return (values * norm_of(values) * INV).astype(BF16)

    def recv_opp(d, carry):
        opp_copy(d).wait_recv()
        return carry

    def recv_own(d, carry):
        own_copy(d).wait_recv()
        return carry

    def slot(s):
        return jnp.maximum(2 * s - 1 + c, 0)

    def hop(s, i):
        rows = pl.ds(pl.multiple_of(i * SR, SR), SR)
        return copy_to(ring.at[slot(s), rows], ring.at[slot(s + 1), rows], ring_s.at[s, i], ring_r.at[s, i], after)

    def jump(i):
        rows = pl.ds(pl.multiple_of(i * SR, SR), SR)
        return copy_to(ring.at[0, rows], ring.at[slot(JUMP), rows], ring_s.at[JUMP - 1, i], ring_r.at[JUMP - 1, i], ahead)

    def share(s):
        return copy_to(ring.at[slot(s)], ring.at[slot(s)], sib_s.at[s], sib_r.at[s], sibling)

    def share_half(s, index):
        rows = pl.ds(pl.multiple_of(c * SL, SL), SL)
        return copy_to(ring.at[index, rows], ring.at[index, rows], sib_s.at[s], sib_r.at[s], sibling)

    def order(i):
        return lax.rem(2 * c + i, SUB)

    lax.fori_loop(0, NM, recv_opp, 0)
    ring[0, pl.ds(pl.multiple_of(c * SL, SL), SL), :] = embed(assemble(opp_in))
    share_half(0, 0).start()
    jump(order(0)).start()
    jump(order(1)).start()
    hop(0, order(0)).start()
    hop(0, order(1)).start()

    lax.fori_loop(1, NM, recv_own, 0)
    own_proj[...] = assemble(own_in)
    own_rows[...] = embed(own_proj[...])

    share_half(0, 0).wait_recv()
    jump(order(2)).start()
    jump(order(3)).start()
    hop(0, order(2)).start()
    hop(0, order(3)).start()

    def emb_copy(dx, dy):
        target = at(k, z, lax.rem(xh + dx, 2), lax.rem(y + dy, NY) * 2 + xh)
        return copy_to(own_rows, own_emb.at[m], emb_s.at[dx, dy], emb_r.at[c, dy], target)

    def emb_wait(core, dy):
        copy_to(own_rows, own_emb.at[0], emb_s.at[0, 0], emb_r.at[core, dy], sibling).wait_recv()

    mine = c == xh

    @pl.when(mine)
    def _():
        own_emb[m] = own_rows[...]

    @pl.when(jnp.logical_not(mine))
    def _():
        emb_copy(0, 0).start()

    for dy in range(1, NY):
        emb_copy(0, dy).start()
    for dy in range(NY):
        emb_copy(1, dy).start()

    strip_copy.start()
    grad[...] = jnp.zeros_like(grad)

    def emb_ready():
        for core in range(2):
            for dy in range(NY):
                if dy == 0:
                    @pl.when(jnp.logical_not(jnp.logical_and(mine, core == c)))
                    def _(core=core):
                        emb_wait(core, 0)
                else:
                    emb_wait(core, dy)

    def forward(s):
        for i in range(SUB):
            hop(s - 1, order(i)).wait_recv()
            hop(s, order(i)).start()
        share(s).start()

    def batch(j):
        opposite = ring[pl.ds(4 * j, 4)].reshape(4 * CH, E)
        own = own_emb[...].reshape(ROWS, E)
        logits = LOGIT_SCALE * lax.dot_general(
            own, opposite, (((1,), (1,)), ((), ())), preferred_element_type=F32
        ) + LOGIT_BIAS
        partner = opp_ids[pl.ds(2 * j, 2), :]
        same = jnp.concatenate([own_ids[...] == partner[0:1], own_ids[...] == partner[1:2]], axis=1)
        sign = jnp.where(same, 1.0, -1.0)
        weights = (-sign / (1.0 + jnp.exp(sign * logits))).astype(BF16)
        grad[...] += jnp.dot(weights, opposite, preferred_element_type=F32)

    def arrived(*steps):
        for step in steps:
            share(step).wait_recv()

    for t in range(1, 4):
        forward(t)
        forward(JUMP - 1 + t)
    emb_ready()
    arrived(1, 2)
    batch(0)
    arrived(JUMP)

    def two_hops(u, carry):
        t = 4 + 2 * u
        forward(t)
        forward(JUMP - 1 + t)
        arrived(JUMP + 2 * u + 1, JUMP + 2 * u + 2)
        batch(JUMP // 2 + u)
        for i in range(SUB):
            hop(t, order(i)).wait_recv()

            @pl.when(u == 0)
            def _(i=i):
                hop(t + 1, order(i)).start()
        share(t + 1).start()
        forward(JUMP + t)
        arrived(2 * u + 3, 2 * u + 4)
        batch(1 + u)
        return carry

    lax.fori_loop(0, 2, two_hops, 0)

    last = HOPS - 1

    def last_hop(i):
        rows = pl.ds(pl.multiple_of(i * SR, SR), SR)
        return copy_to(ring.at[slot(last), rows], ring.at[2 * HOPS - 1, rows],
                       ring_s.at[last, i], ring_r.at[last, i], after)

    for i in range(SUB):
        hop(last - 1, order(i)).wait_recv()
        if i < SUB // 2:
            last_hop(order(i)).start()
    share(last).start()
    arrived(JUMP - 1, HOPS - 3, HOPS - 2)

    def left_over(u, carry):
        batch(JUMP // 2 - 1 + 3 * u)
        return carry

    lax.fori_loop(0, 2, left_over, 0)
    for i in range(SUB // 2):
        last_hop(order(i)).wait_recv()
    share_half(HOPS, 2 * HOPS - 1).start()
    share(last).wait_recv()
    share_half(HOPS, 2 * HOPS - 1).wait_recv()
    batch(HOPS // 2 - 1)

    grad_out[...] = (LOGIT_SCALE * grad[...]).astype(BF16).reshape(NM, SL, E)

    def grad_copy(core, dy):
        unit = lax.rem(y + dy, NY) * 2 + core
        return copy_to(grad_out.at[unit], grad_in.at[xh * NY + dy], grad_s.at[core, dy],
                       grad_r.at[xh, dy], at(k, z, c, unit))

    def grad_wait(half, dy):
        copy_to(grad_out.at[0], grad_in.at[0], grad_s.at[0, 0], grad_r.at[half, dy], sibling).wait_recv()

    def grad_all(act):
        for dy in (2, 1, 3, 0):
            for core in range(2):
                if dy == 0:
                    @pl.when(jnp.logical_not(jnp.logical_and(mine, core == c)))
                    def _(core=core):
                        act(grad_copy(core, 0))
                else:
                    act(grad_copy(core, dy))

    grad_all(lambda copy: copy.start())

    @pl.when(mine)
    def _():
        grad_in[xh * NY] = grad_out[m]

    values = own_proj[...].astype(F32)
    norm = norm_of(values)
    for half in range(2):
        for dy in range(NY):
            if dy == 0:
                @pl.when(jnp.logical_not(jnp.logical_and(mine, xh == half)))
                def _(half=half):
                    grad_wait(half, 0)
            else:
                grad_wait(half, dy)
    gradient = grad_in[0].astype(F32)
    for i in range(1, 2 * NY):
        gradient = gradient + grad_in[i].astype(F32)

    inner = jnp.sum(values * gradient, axis=1, keepdims=True)
    back = (norm * INV * gradient - norm ** 3 * inner * E ** -1.5 * values).astype(BF16)
    for t in range(NM):
        back_out[t] = back[:, t * 128:t * 128 + 256]

    def back_copy(d):
        half, unit = in_plane(d)
        return copy_to(back_out.at[unit], back_in.at[q], back_s.at[d], back_r.at[d], at(k, z, half, unit))

    def send_back(d, carry):
        back_copy(d).start()
        return carry

    def recv_back(d, carry):
        back_copy(d).wait_recv()
        return carry

    lax.fori_loop(1, 2 * NM, send_back, 0)
    back_in[q] = back_out[m]
    strip_copy.wait_recv()
    lax.fori_loop(1, 2 * NM, recv_back, 0)

    own_back = back_in[pl.ds(xh * NM, NM)].reshape(ROWS, 256)
    other_back = back_in[pl.ds((1 - xh) * NM, NM)].reshape(ROWS, 256)
    head_part = jnp.dot(strips[0], own_back, preferred_element_type=F32)
    head_part += jnp.dot(strips[1], other_back, preferred_element_type=F32)
    head_part = pltpu.roll(head_part, lax.rem(256 - (COLS - 128) * m, 256), 1)
    extra = jnp.where(lane < COLS - 128, head_part[:, 128:256], 0.0)
    extra = pltpu.roll(extra, 0, 1, stride=COLS - 128, stride_axis=0)
    extra = jnp.sum(extra.reshape(NZ, PAD // 8, 8, 128), axis=2)
    packed = head_part[:, 0:128].reshape(NZ, PAD, 128)
    r = lax.broadcasted_iota(jnp.int32, (NZ, PAD, 128), 1)
    for g in range(PAD // 8):
        packed = jnp.where(r == STRIP + g, extra[:, g:g + 1, :], packed)
    part_out[...] = packed.reshape(GROUP, GROUPS // 2, 2 * PAD, 128).astype(BF16)
    sum_out[...] = jnp.zeros_like(sum_out)

    low, high = lax.rem(z, GROUP), z // GROUP

    stages = ((0, 1), (1, GROUPS // 2 - 1))

    def part_copy(d, stage):
        place = lax.rem(low + d, GROUP)
        pairs = pl.ds(*stages[stage])
        return copy_to(part_out.at[place, pairs], part_in.at[d - 1, pairs], part_s.at[d, stage], part_r.at[d, stage],
                       at(k, high * GROUP + place, xh, m))

    def send_parts(stage):
        for d in (2, 1, 3):
            part_copy(d, stage).start()

    def add_parts(stage):
        first, count = stages[stage]
        for d in (1, 3, 2):
            part_copy(d, stage).wait_recv()
        summed = part_out[low, first:first + count].astype(F32)
        for d in range(GROUP - 1):
            summed = summed + part_in[d, first:first + count].astype(F32)
        sum_out[2 * first:2 * (first + count), 0:PAD, :] = summed.reshape(2 * count, PAD, 128).astype(BF16)

    def sum_copy(group):
        return copy_to(sum_out.at[group], sum_in.at[high], sum_s.at[group], sum_r.at[high],
                       at(k, group * GROUP + low, xh, m))

    def sum_wait(group):
        copy_to(sum_out.at[group], sum_in.at[group], sum_s.at[group], sum_r.at[group], sibling).wait_recv()

    def others(groups, act):
        for group in groups:
            pl.when(group != high)(lambda group=group: act(group))

    def sent_proj(d, carry):
        opp_copy(d).wait_send()

        @pl.when(d > 0)
        def _():
            own_copy(d).wait_send()
        return carry

    def sent_hops(s, carry):
        for i in range(SUB):
            hop(s, i).wait_send()
        share(s + 1).wait_send()
        return carry

    def sent_back(d, carry):
        back_copy(d).wait_send()
        return carry

    send_parts(0)
    send_parts(1)
    add_parts(0)
    others((0, 1), lambda group: sum_copy(group).start())
    add_parts(1)
    others(range(2, GROUPS), lambda group: sum_copy(group).start())
    lax.fori_loop(0, NM, sent_proj, 0)
    share_half(0, 0).wait_send()
    lax.fori_loop(0, last, sent_hops, 0)
    for i in range(SUB // 2):
        last_hop(order(i)).wait_send()
    share_half(HOPS, 2 * HOPS - 1).wait_send()

    @pl.when(jnp.logical_not(mine))
    def _():
        emb_copy(0, 0).wait_send()

    for dy in range(1, NY):
        emb_copy(0, dy).wait_send()
    for dy in range(NY):
        emb_copy(1, dy).wait_send()
    strip_copy.wait_send()
    grad_all(lambda copy: copy.wait_send())
    lax.fori_loop(1, 2 * NM, sent_back, 0)
    for stage in range(2):
        for d in range(1, GROUP):
            part_copy(d, stage).wait_send()
    sum_in[high] = sum_out[high]
    others(range(GROUPS), sum_wait)
    total = sum_in[0].astype(F32)
    for group in range(1, GROUPS):
        total = total + sum_in[group].astype(F32)
    others(range(GROUPS), lambda group: sum_copy(group).wait_send())
    out_ref[:, 0:128] = total[0:STRIP, :]
    spread = jnp.concatenate(
        [jnp.broadcast_to(total[STRIP + g:STRIP + g + 1, :], (8, 128)) for g in range(PAD // 8)], axis=0
    )
    row = lax.rem(lax.broadcasted_iota(jnp.int32, (PAD, 128), 0), 8)
    tail = spread
    for j in range(1, 8):
        tail = jnp.where(row == j, pltpu.roll(spread, 128 - (COLS - 128) * j, 1), tail)
    out_ref[:, 128:COLS] = tail[0:STRIP, 0:COLS - 128]


def per_device(features, head, caption_ids):
    vmem = pl.BlockSpec(memory_space=pltpu.VMEM)
    flops = 2 * ROWS * D * COLS + 4 * ROWS * NZ * CH * E + 4 * NZ * PAD * ROWS * 256
    out = pl.pallas_call(
        kernel,
        out_shape=jax.ShapeDtypeStruct((STRIP, COLS), F32),
        in_specs=[pl.BlockSpec(memory_space=pl.ANY)] * 3,
        out_specs=vmem,
        scratch_shapes=[
            pltpu.VMEM((ROWS, D), BF16),
            pltpu.VMEM((256, D), BF16),
            pltpu.VMEM((128, 128), jnp.int32),
            pltpu.VMEM((NM, SL, 256), BF16),
            pltpu.VMEM((NM, SL, 256), BF16),
            pltpu.VMEM((NM, SL, 256), BF16),
            pltpu.VMEM((NZ, CH, E), BF16),
            pltpu.VMEM((SL, E), BF16),
            pltpu.VMEM((NM, SL, E), BF16),
            pltpu.VMEM((SL, E), BF16),
            pltpu.VMEM((HOPS, 128), jnp.int32),
            pltpu.VMEM((ROWS, 128), jnp.int32),
            pltpu.VMEM((ROWS, E), F32),
            pltpu.VMEM((NM, SL, E), BF16),
            pltpu.VMEM((2 * NY, SL, E), BF16),
            pltpu.VMEM((2, NZ * PAD, ROWS), BF16),
            pltpu.VMEM((NZ * PAD, ROWS), BF16),
            pltpu.VMEM((NM, SL, 256), BF16),
            pltpu.VMEM((2 * NM, SL, 256), BF16),
            pltpu.VMEM((GROUP, GROUPS // 2, 2 * PAD, 128), BF16),
            pltpu.VMEM((GROUP - 1, GROUPS // 2, 2 * PAD, 128), BF16),
            pltpu.VMEM((GROUPS, 32, 128), BF16),
            pltpu.VMEM((GROUPS, 32, 128), BF16),
            DMA((3,)),
            DMA((2, NM)), DMA((2, NM)),
            DMA((2, NY)), DMA((2, NY)),
            DMA((HOPS, SUB)), DMA((HOPS, SUB)),
            DMA((HOPS + 1,)), DMA((HOPS + 1,)),
            DMA, DMA,
            DMA((2, NY)), DMA((2, NY)),
            DMA((2 * NM,)), DMA((2 * NM,)),
            DMA((GROUP, 2)), DMA((GROUP, 2)),
            DMA((GROUPS,)), DMA((GROUPS,)),
        ],
        compiler_params=pltpu.CompilerParams(
            collective_id=0, has_side_effects=True, vmem_limit_bytes=63 << 20
        ),
        cost_estimate=pl.CostEstimate(flops=flops, bytes_accessed=2 << 20, transcendentals=ROWS * NZ * CH),
    )(features[0], head[0].T, caption_ids.reshape(128, 128))
    return out[None]


def solution(mesh):
    in_specs = (P("tower", "blk", None), P("tower", None, "mp"), P())
    out_specs = P("tower", "blk", "mp")
    return jax.shard_map(
        per_device, mesh=mesh, in_specs=in_specs, out_specs=out_specs, check_vma=False
    )
```
